32 devices in a mesh: dp: 8 (over y, x, core), ctx: 4 (over z).
Axes of the slice: x: 2, y: 2, z: 4, core: 2. Of those that a mesh axis runs over, the one named last changes fastest.
Arguments:
- hidden_states: bfloat16 [768, 8192], P('ctx', 'dp'), may hold values from -160 to 160
- out_grads: bfloat16 [768, 8192], P('ctx', 'dp'), may hold values from -6 to 6
- norm_gain: bfloat16 [1, 8192], P(None, 'dp'), may hold values from 0.25 to 1.75
Outputs:
- a_factor: float32 [8192, 8192], P('ctx', 'dp')
- g_factor: float32 [8192, 8192], P('ctx', 'dp')
The draws below stay inside these ranges and needn't reach their ends.
All inputs are finite; a program needn't handle non-finite values.
Results may differ from the reference program's by a relative error of at most 0.0028.
Values may be sent and summed in bfloat16 or wider, within the bound.
No kernel may reach another device: no remote copies, remote signals or barrier semaphores. Data moves between devices by JAX's collectives and lax.ppermute only.
A program may use at most 64 MiB of HBM per device.

```python
import jax
import jax.numpy as jnp
from jax import lax

D = 8192
TOKENS = 768


def draw_hidden_states(key, part):
    key_base = jax.random.fold_in(key, 11)
    key_rows = jax.random.fold_in(key, 12)
    key_cols = jax.random.fold_in(key, 13)
    position = jnp.arange(D, dtype=jnp.float32) / D
    row_scale = jnp.exp(jax.random.uniform(key_rows, (TOKENS, 1), jnp.float32, jnp.log(0.3), jnp.log(3.0)))
    col_base = jnp.exp(jax.random.uniform(key_cols, (1, D), jnp.float32, jnp.log(0.5), jnp.log(5.0)))
    col_scale = col_base * jnp.sqrt(1.0 + 2.0 * position)[None, :]
    values = jnp.clip(jax.random.normal(key_base, (TOKENS, D), jnp.float32), -4.0, 4.0)
    return (values * row_scale * col_scale).astype(jnp.bfloat16)


def shard_levels(stream_key, extent, cuts, low, largest):
    def one(dim, shards_of):
        heights = jax.random.uniform(jax.random.fold_in(jax.random.fold_in(stream_key, 6), dim), (shards_of,), jnp.float32, low / len(cuts), largest / len(cuts))
        return jnp.repeat(jnp.exp(heights), extent[dim] // shards_of).reshape((-1,) + (1,) * (len(extent) - dim - 1))

    factor_of = one(*cuts[0])
    for cut in cuts[1:]:
        factor_of = factor_of * one(*cut)
    return factor_of


def normal_values(stream_key, shape, width, limit, split=(), kind=jnp.bfloat16):
    loudness = shard_levels(stream_key, shape, split, -0.22, 0.18) if split else 1.0
    values = jax.random.normal(stream_key, shape, jnp.float32) * width * loudness
    return jnp.minimum(jnp.maximum(values, -limit), limit).astype(kind)


def setup_inputs(seed: int = 0) -> dict:
    splits = jax.random.split(jax.random.key(seed), 4)
    hidden_states = draw_hidden_states(jax.random.fold_in(splits[3], 71), 0)
    out_grads = normal_values(splits[1], (TOKENS, D), 1.0, 6.0, ((0, 4), (1, 8)))
    norm_gain = jnp.clip(1.0 + 0.15 * jax.random.normal(splits[2], (1, D), jnp.float32), 0.25, 1.75).astype(jnp.bfloat16)
    return {"hidden_states": hidden_states, "out_grads": out_grads, "norm_gain": norm_gain}


def reference(hidden_states, out_grads, norm_gain):
    wide = hidden_states.astype(jnp.float32)
    inv_rms = lax.rsqrt(lax.optimization_barrier(jnp.mean(wide * wide, axis=1, keepdims=True)) + 1e-05)
    normed = (wide * inv_rms * norm_gain.astype(jnp.float32)).astype(jnp.bfloat16)
    a_factor = jnp.dot(normed.T, normed, preferred_element_type=jnp.float32) / TOKENS
    g_factor = jnp.dot(out_grads.T, out_grads, preferred_element_type=jnp.float32) / TOKENS
    return (a_factor, g_factor)
```

```python
import jax
import jax.numpy as jnp
from jax import lax
from jax.sharding import PartitionSpec as P

EPS = 1e-05
AXES = ("dp", "ctx")


def spread(block, axis, source):
    block = jnp.where(lax.axis_index(axis) == source, block, jnp.zeros_like(block))
    return lax.psum(block, axis)


def gram(left, right):
    return lax.dot_general(
        left, right, (((0,), (0,)), ((), ())), preferred_element_type=jnp.float32
    )


def normalize(hidden_states, sums, norm_gain, features):
    inv_rms = lax.rsqrt(sums / features + EPS)
    return (
        hidden_states.astype(jnp.float32) * inv_rms * norm_gain.astype(jnp.float32)
    ).astype(jnp.bfloat16)


def squares(hidden_states):
    local = hidden_states.astype(jnp.float32)
    return jnp.sum(local * local, axis=1, keepdims=True)


def general(hidden_states, out_grads, norm_gain):
    tokens_all = hidden_states.shape[0] * lax.axis_size("ctx")
    features = hidden_states.shape[1] * lax.axis_size("dp")
    sums = lax.psum(squares(hidden_states), "dp")
    normed = normalize(hidden_states, sums, norm_gain, features)
    blocks_per_stripe = lax.axis_size("dp") // lax.axis_size("ctx")
    first_root = lax.axis_index("ctx") * blocks_per_stripe
    out = []
    for own in (normed, out_grads):
        column = lax.all_gather(own, "ctx", axis=0, tiled=True)
        stripe = jnp.concatenate(
            [spread(column, "dp", first_root + i) for i in range(blocks_per_stripe)],
            axis=1,
        )
        out.append(gram(stripe, column) / tokens_all)
    return tuple(out)


def swap(x, n_dp, n_ctx, partner):
    pairs = []
    for d in range(n_dp):
        for c in range(n_ctx):
            other = partner(d, c)
            if other is not None:
                pairs.append((d * n_ctx + c, other[0] * n_ctx + other[1]))
    return lax.ppermute(x, AXES, pairs)


def square_plane(hidden_states, out_grads, norm_gain):
    n_dp, n_ctx = lax.axis_size("dp"), lax.axis_size("ctx")
    tokens, width = hidden_states.shape
    dp, z = lax.axis_index("dp"), lax.axis_index("ctx")
    role = lax.bitwise_xor(dp // 2, z)
    parity = dp % 2

    def go(x, partner):
        return swap(x, n_dp, n_ctx, partner)

    def core(x):
        return go(x, lambda d, c: (d ^ 1, c))

    def along_x(x):
        return go(x, lambda d, c: (d ^ 2, c))

    def along_y(x):
        return go(x, lambda d, c: (d ^ 4, c))

    def across(x):
        return go(x, lambda d, c: (d ^ 6, c))

    def z1(x):
        return go(x, lambda d, c: (d, c ^ 1))

    def z2(x):
        return go(x, lambda d, c: (d, c ^ 2))

    def z_middle(x):
        return go(x, lambda d, c: (d, 3 - c) if c in (1, 2) else None)

    def gather_z(own):
        b = z2(own)
        a = z1(own)
        middle = z_middle(own)
        ends = z1(b)
        last = jnp.where((z == 1) | (z == 2), middle, ends)
        return [own, a, b, last]

    sums = squares(hidden_states)
    sums = sums + core(sums)
    sums = (sums + along_x(sums)) + (along_y(sums) + across(sums))
    normed = normalize(hidden_states, sums, norm_gain, width * n_dp)

    g = gather_z(out_grads)
    x = gather_z(normed)
    order = [g[0], x[0], g[1], g[2], g[3], x[1], x[2], x[3]]
    half = tokens // 2
    n = len(order)
    rx, ry = [], []
    for r in range(n + 1):
        source = order[min(r, n - 1)]
        low, high = source[:half], source[half:]
        if r == n:
            low, high = high, low
        px = low if r == 0 else jnp.where(role == 0, low, ry[r - 1])
        py = high if r == 0 else jnp.where(role == 0, high, rx[r - 1])
        rx.append(along_x(px))
        ry.append(along_y(py))
    stripes = []
    for c in range(n):
        low, high = order[c][:half], order[c][half:]
        if c < n - 1:
            got_low = lax.select_n(role, low, rx[c], rx[c + 2], ry[c + 1])
            got_high = lax.select_n(role, high, ry[c + 2], ry[c], rx[c + 1])
        else:
            got_low = lax.select_n(role, low, rx[c], ry[c + 1], ry[c + 1])
            got_high = lax.select_n(role, high, rx[c + 1], ry[c], rx[c + 1])
        stripes += [got_low, got_high]

    def factor(picks, chunks):
        mine = jnp.concatenate([s for p in picks for s in stripes[2 * p : 2 * p + 2]], axis=0)
        other = core(mine)
        first = jnp.where(parity == 0, mine, other)
        second = jnp.where(parity == 0, other, mine)
        stripe = jnp.concatenate([first, second], axis=1)
        return gram(stripe, jnp.concatenate(chunks, axis=0)) / (tokens * n_ctx)

    g_factor = factor([0, 2, 3, 4], g)
    a_factor = factor([1, 5, 6, 7], x)
    return a_factor, g_factor


def solution(mesh):
    square = mesh.shape["dp"] == 8 and mesh.shape["ctx"] == 4
    return jax.shard_map(
        square_plane if square else general,
        mesh=mesh,
        in_specs=(P("ctx", "dp"), P("ctx", "dp"), P(None, "dp")),
        out_specs=(P("ctx", "dp"), P("ctx", "dp")),
        check_vma=False,
    )
```

```python
import jax
import jax.numpy as jnp
from jax import lax
from jax.experimental import pallas as pl
from jax.experimental.pallas import tpu as pltpu
from jax.sharding import PartitionSpec as P

EPS = 1e-05
AXES = ("dp", "ctx")


def spread(block, axis, source):
    block = jnp.where(lax.axis_index(axis) == source, block, jnp.zeros_like(block))
    return lax.psum(block, axis)


def gram(left, right):
    return lax.dot_general(
        left, right, (((0,), (0,)), ((), ())), preferred_element_type=jnp.float32
    )


ROWS = 256


def gram_rows_kernel(scale, _place, left, right, *rest):
    rest[-1][...] = scale * lax.dot_general(
        left[...], right[...], (((0,), (0,)), ((), ())), preferred_element_type=jnp.float32
    )


def gram_rows(left, right, place, scale, rows_all, into=None):
    depth, rows = left.shape
    steps = rows // ROWS
    columns = right.shape[1]
    grid = pltpu.PrefetchScalarGridSpec(
        num_scalar_prefetch=1,
        grid=(steps,),
        in_specs=[
            pl.BlockSpec((depth, ROWS), lambda i, place: (0, i)),
            pl.BlockSpec((depth, columns), lambda i, place: (0, 0)),
        ]
        + ([] if into is None else [pl.BlockSpec(memory_space=pl.ANY)]),
        out_specs=pl.BlockSpec((ROWS, columns), lambda i, place: (place[0] * steps + i, 0)),
    )
    return pl.pallas_call(
        lambda *refs: gram_rows_kernel(scale, *refs),
        out_shape=jax.ShapeDtypeStruct((rows_all, columns), jnp.float32),
        grid_spec=grid,
        input_output_aliases={} if into is None else {3: 0},
        compiler_params=pltpu.CompilerParams(vmem_limit_bytes=24 * 1024 * 1024),
        cost_estimate=pl.CostEstimate(
            flops=2 * depth * rows * columns,
            bytes_accessed=4 * rows * columns + 2 * depth * (rows + columns),
            transcendentals=0,
        ),
    )(place, left, right, *([] if into is None else [into]))


def normalize(hidden_states, sums, norm_gain, features):
    inv_rms = lax.rsqrt(sums / features + EPS)
    return (
        hidden_states.astype(jnp.float32) * inv_rms * norm_gain.astype(jnp.float32)
    ).astype(jnp.bfloat16)


def squares(hidden_states):
    local = hidden_states.astype(jnp.float32)
    return jnp.sum(local * local, axis=1, keepdims=True)


def general(hidden_states, out_grads, norm_gain):
    tokens_all = hidden_states.shape[0] * lax.axis_size("ctx")
    features = hidden_states.shape[1] * lax.axis_size("dp")
    sums = lax.psum(squares(hidden_states), "dp")
    normed = normalize(hidden_states, sums, norm_gain, features)
    blocks_per_stripe = lax.axis_size("dp") // lax.axis_size("ctx")
    first_root = lax.axis_index("ctx") * blocks_per_stripe
    out = []
    for own in (normed, out_grads):
        column = lax.all_gather(own, "ctx", axis=0, tiled=True)
        stripe = jnp.concatenate(
            [spread(column, "dp", first_root + i) for i in range(blocks_per_stripe)],
            axis=1,
        )
        out.append(gram(stripe, column) / tokens_all)
    return tuple(out)


def swap(x, n_dp, n_ctx, partner):
    pairs = []
    for d in range(n_dp):
        for c in range(n_ctx):
            other = partner(d, c)
            if other is not None:
                pairs.append((d * n_ctx + c, other[0] * n_ctx + other[1]))
    return lax.ppermute(x, AXES, pairs)


def square_plane(hidden_states, out_grads, norm_gain):
    n_dp, n_ctx = lax.axis_size("dp"), lax.axis_size("ctx")
    tokens, width = hidden_states.shape
    dp, z = lax.axis_index("dp"), lax.axis_index("ctx")
    role = lax.bitwise_xor(dp // 2, z)
    parity = dp % 2

    def go(x, partner):
        return swap(x, n_dp, n_ctx, partner)

    def core(x):
        return go(x, lambda d, c: (d ^ 1, c))

    def along_x(x):
        return go(x, lambda d, c: (d ^ 2, c))

    def along_y(x):
        return go(x, lambda d, c: (d ^ 4, c))

    def across(x):
        return go(x, lambda d, c: (d ^ 6, c))

    def z1(x):
        return go(x, lambda d, c: (d, c ^ 1))

    def z2(x):
        return go(x, lambda d, c: (d, c ^ 2))

    def z_middle(x):
        return go(x, lambda d, c: (d, 3 - c) if c in (1, 2) else None)

    def tie(*values):
        return lax.optimization_barrier(values)

    half = tokens // 2
    root = role == 0

    def send(new, back=None, last=False):
        low, high = (new[half:], new[:half]) if last else (new[:half], new[half:])
        if back is not None:
            low = jnp.where(root, low, back[1])
            high = jnp.where(root, high, back[0])
        return along_x(low), along_y(high)

    def assemble(own, got):
        n = len(own)
        pieces = []
        for c in range(n):
            low, high = own[c][:half], own[c][half:]
            x0, y0 = got[c]
            x1, y1 = got[c + 1]
            if c < n - 1:
                x2, y2 = got[c + 2]
                pieces.append(lax.select_n(role, low, x0, x2, y1))
                pieces.append(lax.select_n(role, high, y2, y0, x1))
            else:
                pieces.append(lax.select_n(role, low, x0, y1, y1))
                pieces.append(lax.select_n(role, high, x1, y0, x1))
        return jnp.concatenate(pieces, axis=0)

    inner = (z == 1) | (z == 2)
    scale = 1.0 / (tokens * n_ctx)
    rows_all = 2 * width
    mine_at = jnp.reshape(parity, (1,)).astype(jnp.int32)
    other_at = 1 - mine_at

    g0 = out_grads
    g2, g1 = z2(g0), z1(g0)
    sums = squares(hidden_states)
    sums = sums + core(sums)
    sums = (sums + along_x(sums)) + (along_y(sums) + across(sums))
    e0 = send(g0)
    x0 = normalize(hidden_states, sums, norm_gain, width * n_dp)
    *e0, x0 = tie(*e0, x0)
    o0 = send(x0)
    x1 = z1(x0)
    g1_, g2_, g0_ = tie(g1, g2, g0)
    g_ends, g_middle = z1(g2_), z_middle(g0_)
    o0x, o0y, e0x, e0y, g1, g2, x0_ = tie(*o0, *e0, g1, g2, x0)
    o0, e0 = (o0x, o0y), (e0x, e0y)
    e1 = send(g1, e0)
    x2 = z2(x0_)
    e1x, e1y, g_ends, g_middle, g2_ = tie(*e1, g_ends, g_middle, g2)
    e1 = (e1x, e1y)
    e2 = send(g2_, e1)
    e2x, e2y, x1, o0x, o0y = tie(*e2, x1, *o0)
    e2, o0 = (e2x, e2y), (o0x, o0y)
    g3 = jnp.where(inner, g_middle, g_ends)
    e3, o1 = send(g3, e2), send(x1, o0)
    x2, x0_ = tie(x2, x0_)
    x_ends, x_middle = z1(x2), z_middle(x0_)
    e3x, e3y, o1x, o1y, x2_ = tie(*e3, *o1, x2)
    e3, o1 = (e3x, e3y), (o1x, o1y)
    e4, o2 = send(g3, e3, last=True), send(x2_, o1)
    e4x, e4y, o2x, o2y, x_ends, x_middle = tie(*e4, *o2, x_ends, x_middle)
    e4, o2 = (e4x, e4y), (o2x, o2y)
    x3 = jnp.where(inner, x_middle, x_ends)
    o3 = send(x3, o2)
    g_mine = assemble([g0, g1, g2, g3], [e0, e1, e2, e3, e4])
    g_other = core(g_mine)
    g_column = jnp.concatenate([g0, g1, g2, g3], axis=0)
    g_factor = gram_rows(g_mine, g_column, mine_at, scale, rows_all)
    o3x, o3y, g_factor, g_other = tie(*o3, g_factor, g_other)
    o3 = (o3x, o3y)
    o4 = send(x3, o3, last=True)
    g_factor = gram_rows(g_other, g_column, other_at, scale, rows_all, g_factor)
    x_column = jnp.concatenate([x0, x1, x2, x3], axis=0)
    o4x, o4y, g_factor, x_column = tie(*o4, g_factor, x_column)
    o4 = (o4x, o4y)
    x_mine = assemble([x0, x1, x2, x3], [o0, o1, o2, o3, o4])
    x_other = core(x_mine)
    a_factor = gram_rows(x_mine, x_column, mine_at, scale, rows_all)
    a_factor = gram_rows(x_other, x_column, other_at, scale, rows_all, a_factor)
    return a_factor, g_factor


def solution(mesh):
    square = mesh.shape["dp"] == 8 and mesh.shape["ctx"] == 4
    return jax.shard_map(
        square_plane if square else general,
        mesh=mesh,
        in_specs=(P("ctx", "dp"), P("ctx", "dp"), P(None, "dp")),
        out_specs=(P("ctx", "dp"), P("ctx", "dp")),
        check_vma=False,
    )
```

```python
import jax
import jax.numpy as jnp
from jax import lax
from jax.experimental import pallas as pl
from jax.experimental.pallas import tpu as pltpu
from jax.sharding import PartitionSpec as P

EPS = 1e-05
AXES = ("dp", "ctx")


def spread(block, axis, source):
    block = jnp.where(lax.axis_index(axis) == source, block, jnp.zeros_like(block))
    return lax.psum(block, axis)


def gram(left, right):
    return lax.dot_general(
        left, right, (((0,), (0,)), ((), ())), preferred_element_type=jnp.float32
    )


ROWS = 512


def gram_rows_kernel(scale, _place, left, right, *rest):
    rest[-1][...] = scale * lax.dot_general(
        left[...], right[...], (((0,), (0,)), ((), ())), preferred_element_type=jnp.float32
    )


def gram_rows(left, right, place, scale, rows_all, into=None):
    depth, rows = left.shape
    steps = rows // ROWS
    columns = right.shape[1]
    grid = pltpu.PrefetchScalarGridSpec(
        num_scalar_prefetch=1,
        grid=(steps,),
        in_specs=[
            pl.BlockSpec((depth, ROWS), lambda i, place: (0, i)),
            pl.BlockSpec((depth, columns), lambda i, place: (0, 0)),
        ]
        + ([] if into is None else [pl.BlockSpec(memory_space=pl.ANY)]),
        out_specs=pl.BlockSpec((ROWS, columns), lambda i, place: (place[0] * steps + i, 0)),
    )
    return pl.pallas_call(
        lambda *refs: gram_rows_kernel(scale, *refs),
        out_shape=jax.ShapeDtypeStruct((rows_all, columns), jnp.float32),
        grid_spec=grid,
        input_output_aliases={} if into is None else {3: 0},
        compiler_params=pltpu.CompilerParams(vmem_limit_bytes=32 * 1024 * 1024),
        cost_estimate=pl.CostEstimate(
            flops=2 * depth * rows * columns,
            bytes_accessed=4 * rows * columns + 2 * depth * (rows + columns),
            transcendentals=0,
        ),
    )(place, left, right, *([] if into is None else [into]))


def normalize(hidden_states, sums, norm_gain, features):
    inv_rms = lax.rsqrt(sums / features + EPS)
    return (
        hidden_states.astype(jnp.float32) * inv_rms * norm_gain.astype(jnp.float32)
    ).astype(jnp.bfloat16)


def squares(hidden_states):
    local = hidden_states.astype(jnp.float32)
    return jnp.sum(local * local, axis=1, keepdims=True)


def general(hidden_states, out_grads, norm_gain):
    tokens_all = hidden_states.shape[0] * lax.axis_size("ctx")
    features = hidden_states.shape[1] * lax.axis_size("dp")
    sums = lax.psum(squares(hidden_states), "dp")
    normed = normalize(hidden_states, sums, norm_gain, features)
    blocks_per_stripe = lax.axis_size("dp") // lax.axis_size("ctx")
    first_root = lax.axis_index("ctx") * blocks_per_stripe
    out = []
    for own in (normed, out_grads):
        column = lax.all_gather(own, "ctx", axis=0, tiled=True)
        stripe = jnp.concatenate(
            [spread(column, "dp", first_root + i) for i in range(blocks_per_stripe)],
            axis=1,
        )
        out.append(gram(stripe, column) / tokens_all)
    return tuple(out)


def swap(x, n_dp, n_ctx, partner):
    pairs = []
    for d in range(n_dp):
        for c in range(n_ctx):
            other = partner(d, c)
            if other is not None:
                pairs.append((d * n_ctx + c, other[0] * n_ctx + other[1]))
    return lax.ppermute(x, AXES, pairs)


def square_plane(hidden_states, out_grads, norm_gain):
    n_dp, n_ctx = lax.axis_size("dp"), lax.axis_size("ctx")
    tokens, width = hidden_states.shape
    dp, z = lax.axis_index("dp"), lax.axis_index("ctx")
    role = lax.bitwise_xor(dp // 2, z)
    parity = dp % 2

    def go(x, partner):
        return swap(x, n_dp, n_ctx, partner)

    def core(x):
        return go(x, lambda d, c: (d ^ 1, c))

    def along_x(x):
        return go(x, lambda d, c: (d ^ 2, c))

    def along_y(x):
        return go(x, lambda d, c: (d ^ 4, c))

    def across(x):
        return go(x, lambda d, c: (d ^ 6, c))

    ring = (0, 1, 3, 2)

    def along_z(x):
        return go(x, lambda d, c: (d, ring[(ring.index(c) + 1) % 4]))

    def tie(*values):
        return lax.optimization_barrier(values)

    half = tokens // 2
    root = role == 0

    def send(new, back=None, last=False):
        low, high = (new[half:], new[:half]) if last else (new[:half], new[half:])
        if back is not None:
            low = jnp.where(root, low, back[1])
            high = jnp.where(root, high, back[0])
        return along_x(low), along_y(high)

    def assemble(own, got):
        n = len(own)
        pieces = []
        for c in range(n):
            low, high = own[c][:half], own[c][half:]
            x0, y0 = got[c]
            x1, y1 = got[c + 1]
            if c < n - 1:
                x2, y2 = got[c + 2]
                pieces.append(lax.select_n(role, low, x0, x2, y1))
                pieces.append(lax.select_n(role, high, y2, y0, x1))
            else:
                pieces.append(lax.select_n(role, low, x0, y1, y1))
                pieces.append(lax.select_n(role, high, x1, y0, x1))
        return jnp.concatenate(pieces, axis=0)

    scale = 1.0 / (tokens * n_ctx)
    rows_all = 2 * width
    mine_at = jnp.reshape(parity, (1,)).astype(jnp.int32)
    other_at = 1 - mine_at

    g0 = out_grads
    g1 = along_z(g0)
    sums = squares(hidden_states)
    sums = sums + core(sums)
    sums = (sums + along_x(sums)) + (along_y(sums) + across(sums))
    e0 = send(g0)
    x0 = normalize(hidden_states, sums, norm_gain, width * n_dp)
    e0x, e0y = e0
    x0, g1 = tie(x0, g1)
    g2 = along_z(g1)
    o0x, o0y = send(x0)
    x1 = along_z(x0)
    g3 = along_z(g2)
    o0x, o0y, e0x, e0y, g1, g2 = tie(o0x, o0y, e0x, e0y, g1, g2)
    e1x, e1y = send(g1, (e0x, e0y))
    e1x, e1y, g2, x1 = tie(e1x, e1y, g2, x1)
    x2 = along_z(x1)
    e2x, e2y = send(g2, (e1x, e1y))
    e2x, e2y, o0x, o0y, g3 = tie(e2x, e2y, o0x, o0y, g3)
    e3x, e3y = send(g3, (e2x, e2y))
    o1x, o1y = send(x1, (o0x, o0y))
    e3x, e3y, o1x, o1y, x2 = tie(e3x, e3y, o1x, o1y, x2)
    x3 = along_z(x2)
    e4x, e4y = send(g3, (e3x, e3y), last=True)
    o2x, o2y = send(x2, (o1x, o1y))
    e4x, e4y, o2x, o2y, x3, g1, g2, g3 = tie(e4x, e4y, o2x, o2y, x3, g1, g2, g3)
    o3x, o3y = send(x3, (o2x, o2y))
    g_mine = assemble([g0, g1, g2, g3], [(e0x, e0y), (e1x, e1y), (e2x, e2y), (e3x, e3y), (e4x, e4y)])
    g_other = core(g_mine)
    g_column = jnp.concatenate([g0, g1, g2, g3], axis=0)
    g_factor = gram_rows(g_mine, g_column, mine_at, scale, rows_all)
    o3x, o3y, g_factor, x0, x1, x2, x3, g_other = tie(o3x, o3y, g_factor, x0, x1, x2, x3, g_other)
    o4x, o4y = send(x3, (o3x, o3y), last=True)
    g_factor = gram_rows(g_other, g_column, other_at, scale, rows_all, g_factor)
    x_column = jnp.concatenate([x0, x1, x2, x3], axis=0)
    o4x, o4y, g_factor, x_column = tie(o4x, o4y, g_factor, x_column)
    x_mine = assemble([x0, x1, x2, x3], [(o0x, o0y), (o1x, o1y), (o2x, o2y), (o3x, o3y), (o4x, o4y)])
    x_other = core(x_mine)
    a_factor = gram_rows(x_mine, x_column, mine_at, scale, rows_all)
    a_factor = gram_rows(x_other, x_column, other_at, scale, rows_all, a_factor)
    return a_factor, g_factor


def solution(mesh):
    square = mesh.shape["dp"] == 8 and mesh.shape["ctx"] == 4
    return jax.shard_map(
        square_plane if square else general,
        mesh=mesh,
        in_specs=(P("ctx", "dp"), P("ctx", "dp"), P(None, "dp")),
        out_specs=(P("ctx", "dp"), P("ctx", "dp")),
        check_vma=False,
    )
```

```python
import jax
import jax.numpy as jnp
from jax import lax
from jax.experimental import pallas as pl
from jax.experimental.pallas import tpu as pltpu
from jax.sharding import PartitionSpec as P

EPS = 1e-05
AXES = ("dp", "ctx")


def spread(block, axis, source):
    block = jnp.where(lax.axis_index(axis) == source, block, jnp.zeros_like(block))
    return lax.psum(block, axis)


def gram(left, right):
    return lax.dot_general(
        left, right, (((0,), (0,)), ((), ())), preferred_element_type=jnp.float32
    )


ROWS = 512


def gram_rows_kernel(scale, _place, left, right, *rest):
    rest[-1][...] = scale * lax.dot_general(
        left[...], right[...], (((0,), (0,)), ((), ())), preferred_element_type=jnp.float32
    )


def gram_rows(left, right, place, scale, rows_all, into=None):
    depth, rows = left.shape
    steps = rows // ROWS
    columns = right.shape[1]
    grid = pltpu.PrefetchScalarGridSpec(
        num_scalar_prefetch=1,
        grid=(steps,),
        in_specs=[
            pl.BlockSpec((depth, ROWS), lambda i, place: (0, i)),
            pl.BlockSpec((depth, columns), lambda i, place: (0, 0)),
        ]
        + ([] if into is None else [pl.BlockSpec(memory_space=pl.ANY)]),
        out_specs=pl.BlockSpec((ROWS, columns), lambda i, place: (place[0] * steps + i, 0)),
    )
    return pl.pallas_call(
        lambda *refs: gram_rows_kernel(scale, *refs),
        out_shape=jax.ShapeDtypeStruct((rows_all, columns), jnp.float32),
        grid_spec=grid,
        input_output_aliases={} if into is None else {3: 0},
        compiler_params=pltpu.CompilerParams(vmem_limit_bytes=32 * 1024 * 1024),
        cost_estimate=pl.CostEstimate(
            flops=2 * depth * rows * columns,
            bytes_accessed=4 * rows * columns + 2 * depth * (rows + columns),
            transcendentals=0,
        ),
    )(place, left, right, *([] if into is None else [into]))


def normalize(hidden_states, sums, norm_gain, features):
    inv_rms = lax.rsqrt(sums / features + EPS)
    return (
        hidden_states.astype(jnp.float32) * inv_rms * norm_gain.astype(jnp.float32)
    ).astype(jnp.bfloat16)


def squares(hidden_states):
    local = hidden_states.astype(jnp.float32)
    return jnp.sum(local * local, axis=1, keepdims=True)


def general(hidden_states, out_grads, norm_gain):
    tokens_all = hidden_states.shape[0] * lax.axis_size("ctx")
    features = hidden_states.shape[1] * lax.axis_size("dp")
    sums = lax.psum(squares(hidden_states), "dp")
    normed = normalize(hidden_states, sums, norm_gain, features)
    blocks_per_stripe = lax.axis_size("dp") // lax.axis_size("ctx")
    first_root = lax.axis_index("ctx") * blocks_per_stripe
    out = []
    for own in (normed, out_grads):
        column = lax.all_gather(own, "ctx", axis=0, tiled=True)
        stripe = jnp.concatenate(
            [spread(column, "dp", first_root + i) for i in range(blocks_per_stripe)],
            axis=1,
        )
        out.append(gram(stripe, column) / tokens_all)
    return tuple(out)


def swap(x, n_dp, n_ctx, partner):
    pairs = []
    for d in range(n_dp):
        for c in range(n_ctx):
            other = partner(d, c)
            if other is not None:
                pairs.append((d * n_ctx + c, other[0] * n_ctx + other[1]))
    return lax.ppermute(x, AXES, pairs)


def square_plane(hidden_states, out_grads, norm_gain):
    n_dp, n_ctx = lax.axis_size("dp"), lax.axis_size("ctx")
    tokens, width = hidden_states.shape
    dp, z = lax.axis_index("dp"), lax.axis_index("ctx")
    role = lax.bitwise_xor(dp // 2, z)
    parity = dp % 2

    def go(x, partner):
        return swap(x, n_dp, n_ctx, partner)

    def core(x):
        return go(x, lambda d, c: (d ^ 1, c))

    def along_x(x):
        return go(x, lambda d, c: (d ^ 2, c))

    def along_y(x):
        return go(x, lambda d, c: (d ^ 4, c))

    def across(x):
        return go(x, lambda d, c: (d ^ 6, c))

    ring = (0, 1, 3, 2)

    def along_z(x, step):
        return go(x, lambda d, c: (d, ring[(ring.index(c) + step) % 4]))

    def tie(*values):
        return lax.optimization_barrier(values)

    half = tokens // 2
    root = role == 0

    def send(new, back=None, last=False):
        low, high = (new[half:], new[:half]) if last else (new[:half], new[half:])
        if back is not None:
            low = jnp.where(root, low, back[1])
            high = jnp.where(root, high, back[0])
        return along_x(low), along_y(high)

    def assemble(picks, chunks, got):
        pieces = []
        for c, chunk in zip(picks, chunks):
            low, high = chunk[:half], chunk[half:]
            x0, y0 = got[c]
            x1, y1 = got[c + 1]
            if c + 2 < len(got):
                x2, y2 = got[c + 2]
                pieces.append(lax.select_n(role, low, x0, x2, y1))
                pieces.append(lax.select_n(role, high, y2, y0, x1))
            else:
                pieces.append(lax.select_n(role, low, x0, y1, y1))
                pieces.append(lax.select_n(role, high, x1, y0, x1))
        return jnp.concatenate(pieces, axis=0)

    scale = 1.0 / (tokens * n_ctx)
    rows_all = 2 * width
    mine_at = jnp.reshape(parity, (1,)).astype(jnp.int32)
    other_at = 1 - mine_at

    g0 = out_grads
    g1 = along_z(g0, 1)
    r0x, r0y = send(g0)
    sums = squares(hidden_states)
    sums = sums + core(sums)
    sums = (sums + along_x(sums)) + (along_y(sums) + across(sums))
    x0 = normalize(hidden_states, sums, norm_gain, width * n_dp)
    r0x, r0y, g1 = tie(r0x, r0y, g1)
    r1x, r1y = send(g1, (r0x, r0y))
    x1 = along_z(x0, 1)
    g2 = along_z(g1, 1)
    g3 = along_z(g2, 1)
    r1x, r1y, g2 = tie(r1x, r1y, g2)
    r2x, r2y = send(g2, (r1x, r1y))
    r2x, r2y, x0 = tie(r2x, r2y, x0)
    r3x, r3y = send(x0, (r2x, r2y))
    x2 = along_z(x1, 1)
    r3x, r3y, g3 = tie(r3x, r3y, g3)
    r4x, r4y = send(g3, (r3x, r3y))
    r4x, r4y, x1 = tie(r4x, r4y, x1)
    r5x, r5y = send(x1, (r4x, r4y))
    x3 = along_z(x2, 1)
    r5x, r5y, x2 = tie(r5x, r5y, x2)
    r6x, r6y = send(x2, (r5x, r5y))
    r6x, r6y, x3 = tie(r6x, r6y, x3)
    r7x, r7y = send(x3, (r6x, r6y))
    g_mine = assemble([0, 1, 2, 4], [g0, g1, g2, g3], [(r0x, r0y), (r1x, r1y), (r2x, r2y), (r3x, r3y), (r4x, r4y), (r5x, r5y), (r6x, r6y)])
    g_other = core(g_mine)
    g_column = jnp.concatenate([g0, g1, g2, g3], axis=0)
    g_factor = gram_rows(g_mine, g_column, mine_at, scale, rows_all)
    r7x, r7y, g_factor, g_other, x0, x1, x2, x3 = tie(r7x, r7y, g_factor, g_other, x0, x1, x2, x3)
    r8x, r8y = send(x3, (r7x, r7y), last=True)
    g_factor = gram_rows(g_other, g_column, other_at, scale, rows_all, g_factor)
    x_column = jnp.concatenate([x0, x1, x2, x3], axis=0)
    r8x, r8y, x_column, g_factor = tie(r8x, r8y, x_column, g_factor)
    x_mine = assemble([3, 5, 6, 7], [x0, x1, x2, x3], [(r0x, r0y), (r1x, r1y), (r2x, r2y), (r3x, r3y), (r4x, r4y), (r5x, r5y), (r6x, r6y), (r7x, r7y), (r8x, r8y)])
    x_other = core(x_mine)
    a_factor = gram_rows(x_mine, x_column, mine_at, scale, rows_all)
    a_factor = gram_rows(x_other, x_column, other_at, scale, rows_all, a_factor)
    return a_factor, g_factor


def solution(mesh):
    square = mesh.shape["dp"] == 8 and mesh.shape["ctx"] == 4
    return jax.shard_map(
        square_plane if square else general,
        mesh=mesh,
        in_specs=(P("ctx", "dp"), P("ctx", "dp"), P(None, "dp")),
        out_specs=(P("ctx", "dp"), P("ctx", "dp")),
        check_vma=False,
    )
```

```python
import jax
import jax.numpy as jnp
from jax import lax
from jax.experimental import pallas as pl
from jax.experimental.pallas import tpu as pltpu
from jax.sharding import PartitionSpec as P

EPS = 1e-05
AXES = ("dp", "ctx")


def spread(block, axis, source):
    block = jnp.where(lax.axis_index(axis) == source, block, jnp.zeros_like(block))
    return lax.psum(block, axis)


def gram(left, right):
    return lax.dot_general(
        left, right, (((0,), (0,)), ((), ())), preferred_element_type=jnp.float32
    )


ROWS = 512


def gram_rows_kernel(scale, count, _place, left, *refs):
    column = jnp.concatenate([ref[...] for ref in refs[:count]], axis=0)
    refs[-1][...] = scale * lax.dot_general(
        left[...], column, (((0,), (0,)), ((), ())), preferred_element_type=jnp.float32
    )


def gram_rows(left, chunks, place, scale, rows_all, into=None):
    depth, rows = left.shape
    steps = rows // ROWS
    columns = chunks[0].shape[1]
    grid = pltpu.PrefetchScalarGridSpec(
        num_scalar_prefetch=1,
        grid=(steps,),
        in_specs=[pl.BlockSpec((depth, ROWS), lambda i, place: (0, i))]
        + [pl.BlockSpec(chunk.shape, lambda i, place: (0, 0)) for chunk in chunks]
        + ([] if into is None else [pl.BlockSpec(memory_space=pl.ANY)]),
        out_specs=pl.BlockSpec((ROWS, columns), lambda i, place: (place[0] * steps + i, 0)),
    )
    return pl.pallas_call(
        lambda *refs: gram_rows_kernel(scale, len(chunks), *refs),
        out_shape=jax.ShapeDtypeStruct((rows_all, columns), jnp.float32),
        grid_spec=grid,
        input_output_aliases={} if into is None else {2 + len(chunks): 0},
        compiler_params=pltpu.CompilerParams(vmem_limit_bytes=32 * 1024 * 1024),
        cost_estimate=pl.CostEstimate(
            flops=2 * depth * rows * columns,
            bytes_accessed=4 * rows * columns + 2 * depth * (rows + columns),
            transcendentals=0,
        ),
    )(place, left, *chunks, *([] if into is None else [into]))


def normalize(hidden_states, sums, norm_gain, features):
    inv_rms = lax.rsqrt(sums / features + EPS)
    return (
        hidden_states.astype(jnp.float32) * inv_rms * norm_gain.astype(jnp.float32)
    ).astype(jnp.bfloat16)


def squares(hidden_states):
    local = hidden_states.astype(jnp.float32)
    return jnp.sum(local * local, axis=1, keepdims=True)


def general(hidden_states, out_grads, norm_gain):
    tokens_all = hidden_states.shape[0] * lax.axis_size("ctx")
    features = hidden_states.shape[1] * lax.axis_size("dp")
    sums = lax.psum(squares(hidden_states), "dp")
    normed = normalize(hidden_states, sums, norm_gain, features)
    blocks_per_stripe = lax.axis_size("dp") // lax.axis_size("ctx")
    first_root = lax.axis_index("ctx") * blocks_per_stripe
    out = []
    for own in (normed, out_grads):
        column = lax.all_gather(own, "ctx", axis=0, tiled=True)
        stripe = jnp.concatenate(
            [spread(column, "dp", first_root + i) for i in range(blocks_per_stripe)],
            axis=1,
        )
        out.append(gram(stripe, column) / tokens_all)
    return tuple(out)


def swap(x, n_dp, n_ctx, partner):
    pairs = []
    for d in range(n_dp):
        for c in range(n_ctx):
            other = partner(d, c)
            if other is not None:
                pairs.append((d * n_ctx + c, other[0] * n_ctx + other[1]))
    return lax.ppermute(x, AXES, pairs)


def square_plane(hidden_states, out_grads, norm_gain):
    n_dp, n_ctx = lax.axis_size("dp"), lax.axis_size("ctx")
    tokens, width = hidden_states.shape
    dp, z = lax.axis_index("dp"), lax.axis_index("ctx")
    role = lax.bitwise_xor(dp // 2, z)
    parity = dp % 2

    def go(x, partner):
        return swap(x, n_dp, n_ctx, partner)

    def core(x):
        return go(x, lambda d, c: (d ^ 1, c))

    def along_x(x):
        return go(x, lambda d, c: (d ^ 2, c))

    def along_y(x):
        return go(x, lambda d, c: (d ^ 4, c))

    def across(x):
        return go(x, lambda d, c: (d ^ 6, c))

    ring = (0, 1, 3, 2)

    def along_z(x, step):
        return go(x, lambda d, c: (d, ring[(ring.index(c) + step) % 4]))

    def tie(*values):
        return lax.optimization_barrier(values)

    half = tokens // 2
    root = role == 0

    def send(new, back=None, last=False):
        low, high = (new[half:], new[:half]) if last else (new[:half], new[half:])
        if back is not None:
            low = jnp.where(root, low, back[1])
            high = jnp.where(root, high, back[0])
        return along_x(low), along_y(high)

    def assemble(picks, chunks, got):
        pieces = []
        for c, chunk in zip(picks, chunks):
            low, high = chunk[:half], chunk[half:]
            x0, y0 = got[c]
            x1, y1 = got[c + 1]
            if c + 2 < len(got):
                x2, y2 = got[c + 2]
                pieces.append(lax.select_n(role, low, x0, x2, y1))
                pieces.append(lax.select_n(role, high, y2, y0, x1))
            else:
                pieces.append(lax.select_n(role, low, x0, y1, y1))
                pieces.append(lax.select_n(role, high, x1, y0, x1))
        return jnp.concatenate(pieces, axis=0)

    scale = 1.0 / (tokens * n_ctx)
    rows_all = 2 * width
    mine_at = jnp.reshape(parity, (1,)).astype(jnp.int32)
    other_at = 1 - mine_at

    g0 = out_grads
    g1 = along_z(g0, 3)
    r0x, r0y = send(g0)
    sums = squares(hidden_states)
    sums = sums + core(sums)
    sums = (sums + along_x(sums)) + (along_y(sums) + across(sums))
    x0 = normalize(hidden_states, sums, norm_gain, width * n_dp)
    r0x, r0y, g1 = tie(r0x, r0y, g1)
    r1x, r1y = send(g1, (r0x, r0y))
    x1 = along_z(x0, 3)
    g2 = along_z(g1, 3)
    r1x, r1y, g2 = tie(r1x, r1y, g2)
    r2x, r2y = send(g2, (r1x, r1y))
    g3 = along_z(g2, 3)
    r2x, r2y, x0 = tie(r2x, r2y, x0)
    r3x, r3y = send(x0, (r2x, r2y))
    x2 = along_z(x1, 3)
    r3x, r3y, g3 = tie(r3x, r3y, g3)
    r4x, r4y = send(g3, (r3x, r3y))
    r4x, r4y, x1 = tie(r4x, r4y, x1)
    r5x, r5y = send(x1, (r4x, r4y))
    x3 = along_z(x2, 3)
    r5x, r5y, x2 = tie(r5x, r5y, x2)
    r6x, r6y = send(x2, (r5x, r5y))
    r6x, r6y, x3, g1, g2, g3 = tie(r6x, r6y, x3, g1, g2, g3)
    r7x, r7y = send(x3, (r6x, r6y))
    g_mine = assemble([0, 1, 2, 4], [g0, g1, g2, g3], [(r0x, r0y), (r1x, r1y), (r2x, r2y), (r3x, r3y), (r4x, r4y), (r5x, r5y), (r6x, r6y)])
    g_other = core(g_mine)
    g_column = jnp.concatenate([g1, g2, g3], axis=0)
    g_factor = gram_rows(g_mine, [g0, g_column], mine_at, scale, rows_all)
    r7x, r7y, g_factor, g_other = tie(r7x, r7y, g_factor, g_other)
    r8x, r8y = send(x3, (r7x, r7y), last=True)
    g_factor = gram_rows(g_other, [g0, g_column], other_at, scale, rows_all, g_factor)
    x_column = jnp.concatenate([x0, x1, x2, x3], axis=0)
    r8x, r8y, x_column, g_factor = tie(r8x, r8y, x_column, g_factor)
    x_mine = assemble([3, 5, 6, 7], [x0, x1, x2, x3], [(r0x, r0y), (r1x, r1y), (r2x, r2y), (r3x, r3y), (r4x, r4y), (r5x, r5y), (r6x, r6y), (r7x, r7y), (r8x, r8y)])
    x_other = core(x_mine)
    a_factor = gram_rows(x_mine, [x_column], mine_at, scale, rows_all)
    a_factor = gram_rows(x_other, [x_column], other_at, scale, rows_all, a_factor)
    return a_factor, g_factor


def solution(mesh):
    square = mesh.shape["dp"] == 8 and mesh.shape["ctx"] == 4
    return jax.shard_map(
        square_plane if square else general,
        mesh=mesh,
        in_specs=(P("ctx", "dp"), P("ctx", "dp"), P(None, "dp")),
        out_specs=(P("ctx", "dp"), P("ctx", "dp")),
        check_vma=False,
    )
```

```python
import jax
import jax.numpy as jnp
from jax import lax
from jax.experimental import pallas as pl
from jax.experimental.pallas import tpu as pltpu
from jax.sharding import PartitionSpec as P

EPS = 1e-05
AXES = ("dp", "ctx")


def spread(block, axis, source):
    block = jnp.where(lax.axis_index(axis) == source, block, jnp.zeros_like(block))
    return lax.psum(block, axis)


def gram(left, right):
    return lax.dot_general(
        left, right, (((0,), (0,)), ((), ())), preferred_element_type=jnp.float32
    )


TILES = (8, 4, 4)


def gram_rows_kernel(scale, count, place, left, *refs):
    out, tiles, sems = refs[-3:]
    column = jnp.concatenate([ref[...] for ref in refs[:count]], axis=0)
    rows = left.shape[1]
    base = pl.multiple_of(place[0] * rows, rows)
    copies, start = [], 0
    for part, size in enumerate(TILES):
        size = size * rows // 16
        tiles[pl.ds(start, size)] = scale * lax.dot_general(
            left[:, pl.ds(start, size)], column, (((0,), (0,)), ((), ())), preferred_element_type=jnp.float32
        )
        copies.append(
            pltpu.make_async_copy(tiles.at[pl.ds(start, size)], out.at[pl.ds(base + start, size)], sems.at[part])
        )
        copies[-1].start()
        start += size
    for copy in copies:
        copy.wait()


def gram_rows(left, chunks, place, scale, rows_all, into=None):
    depth, rows = left.shape
    columns = chunks[0].shape[1]
    return pl.pallas_call(
        lambda *refs: gram_rows_kernel(scale, len(chunks), *refs),
        out_shape=jax.ShapeDtypeStruct((rows_all, columns), jnp.float32),
        in_specs=[pl.BlockSpec(memory_space=pltpu.SMEM)]
        + [pl.BlockSpec(memory_space=pltpu.VMEM)] * (1 + len(chunks))
        + ([] if into is None else [pl.BlockSpec(memory_space=pl.ANY)]),
        out_specs=pl.BlockSpec(memory_space=pl.ANY),
        scratch_shapes=[pltpu.VMEM((rows, columns), jnp.float32), pltpu.SemaphoreType.DMA((len(TILES),))],
        input_output_aliases={} if into is None else {2 + len(chunks): 0},
        compiler_params=pltpu.CompilerParams(vmem_limit_bytes=32 * 1024 * 1024),
        cost_estimate=pl.CostEstimate(
            flops=2 * depth * rows * columns,
            bytes_accessed=4 * rows * columns + 2 * depth * (rows + columns),
            transcendentals=0,
        ),
    )(place, left, *chunks, *([] if into is None else [into]))


def normalize(hidden_states, sums, norm_gain, features):
    inv_rms = lax.rsqrt(sums / features + EPS)
    return (
        hidden_states.astype(jnp.float32) * inv_rms * norm_gain.astype(jnp.float32)
    ).astype(jnp.bfloat16)


def squares(hidden_states):
    local = hidden_states.astype(jnp.float32)
    return jnp.sum(local * local, axis=1, keepdims=True)


def general(hidden_states, out_grads, norm_gain):
    tokens_all = hidden_states.shape[0] * lax.axis_size("ctx")
    features = hidden_states.shape[1] * lax.axis_size("dp")
    sums = lax.psum(squares(hidden_states), "dp")
    normed = normalize(hidden_states, sums, norm_gain, features)
    blocks_per_stripe = lax.axis_size("dp") // lax.axis_size("ctx")
    first_root = lax.axis_index("ctx") * blocks_per_stripe
    out = []
    for own in (normed, out_grads):
        column = lax.all_gather(own, "ctx", axis=0, tiled=True)
        stripe = jnp.concatenate(
            [spread(column, "dp", first_root + i) for i in range(blocks_per_stripe)],
            axis=1,
        )
        out.append(gram(stripe, column) / tokens_all)
    return tuple(out)


def swap(x, n_dp, n_ctx, partner):
    pairs = []
    for d in range(n_dp):
        for c in range(n_ctx):
            other = partner(d, c)
            if other is not None:
                pairs.append((d * n_ctx + c, other[0] * n_ctx + other[1]))
    return lax.ppermute(x, AXES, pairs)


def square_plane(hidden_states, out_grads, norm_gain):
    n_dp, n_ctx = lax.axis_size("dp"), lax.axis_size("ctx")
    tokens, width = hidden_states.shape
    dp, z = lax.axis_index("dp"), lax.axis_index("ctx")
    role = lax.bitwise_xor(dp // 2, z)
    parity = dp % 2

    def go(x, partner):
        return swap(x, n_dp, n_ctx, partner)

    def core(x):
        return go(x, lambda d, c: (d ^ 1, c))

    def along_x(x):
        return go(x, lambda d, c: (d ^ 2, c))

    def along_y(x):
        return go(x, lambda d, c: (d ^ 4, c))

    def across(x):
        return go(x, lambda d, c: (d ^ 6, c))

    ring = (0, 1, 3, 2)

    def along_z(x, step):
        return go(x, lambda d, c: (d, ring[(ring.index(c) + step) % 4]))

    def tie(*values):
        return lax.optimization_barrier(values)

    half = tokens // 2
    root = role == 0

    def send(new, back=None, last=False):
        low, high = (new[half:], new[:half]) if last else (new[:half], new[half:])
        if back is not None:
            low = jnp.where(root, low, back[1])
            high = jnp.where(root, high, back[0])
        return along_x(low), along_y(high)

    def assemble(picks, chunks, got):
        pieces = []
        for c, chunk in zip(picks, chunks):
            low, high = chunk[:half], chunk[half:]
            x0, y0 = got[c]
            x1, y1 = got[c + 1]
            if c + 2 < len(got):
                x2, y2 = got[c + 2]
                pieces.append(lax.select_n(role, low, x0, x2, y1))
                pieces.append(lax.select_n(role, high, y2, y0, x1))
            else:
                pieces.append(lax.select_n(role, low, x0, y1, y1))
                pieces.append(lax.select_n(role, high, x1, y0, x1))
        return jnp.concatenate(pieces, axis=0)

    scale = 1.0 / (tokens * n_ctx)
    rows_all = 2 * width
    mine_at = jnp.reshape(parity, (1,)).astype(jnp.int32)
    other_at = 1 - mine_at

    g0 = out_grads
    g1 = along_z(g0, 3)
    r0x, r0y = send(g0)
    sums = squares(hidden_states)
    sums = sums + core(sums)
    sums = (sums + along_x(sums)) + (along_y(sums) + across(sums))
    x0 = normalize(hidden_states, sums, norm_gain, width * n_dp)
    r0x, r0y, g1 = tie(r0x, r0y, g1)
    r1x, r1y = send(g1, (r0x, r0y))
    x1 = along_z(x0, 3)
    g2 = along_z(g1, 3)
    r1x, r1y, g2 = tie(r1x, r1y, g2)
    r2x, r2y = send(g2, (r1x, r1y))
    g3 = along_z(g2, 3)
    r2x, r2y, x0 = tie(r2x, r2y, x0)
    r3x, r3y = send(x0, (r2x, r2y))
    x2 = along_z(x1, 3)
    r3x, r3y, g3 = tie(r3x, r3y, g3)
    r4x, r4y = send(g3, (r3x, r3y))
    r4x, r4y, x1 = tie(r4x, r4y, x1)
    r5x, r5y = send(x1, (r4x, r4y))
    x3 = along_z(x2, 3)
    r5x, r5y, x2 = tie(r5x, r5y, x2)
    r6x, r6y = send(x2, (r5x, r5y))
    r6x, r6y, x3, g1, g2, g3 = tie(r6x, r6y, x3, g1, g2, g3)
    r7x, r7y = send(x3, (r6x, r6y))
    g_mine = assemble([0, 1, 2, 4], [g0, g1, g2, g3], [(r0x, r0y), (r1x, r1y), (r2x, r2y), (r3x, r3y), (r4x, r4y), (r5x, r5y), (r6x, r6y)])
    g_other = core(g_mine)
    g_column = jnp.concatenate([g1, g2, g3], axis=0)
    g_factor = gram_rows(g_mine, [g0, g_column], mine_at, scale, rows_all)
    r7x, r7y, g_factor, g_other = tie(r7x, r7y, g_factor, g_other)
    r8x, r8y = send(x3, (r7x, r7y), last=True)
    g_factor = gram_rows(g_other, [g0, g_column], other_at, scale, rows_all, g_factor)
    x_column = jnp.concatenate([x0, x1, x2, x3], axis=0)
    r8x, r8y, x_column, g_factor = tie(r8x, r8y, x_column, g_factor)
    x_mine = assemble([3, 5, 6, 7], [x0, x1, x2, x3], [(r0x, r0y), (r1x, r1y), (r2x, r2y), (r3x, r3y), (r4x, r4y), (r5x, r5y), (r6x, r6y), (r7x, r7y), (r8x, r8y)])
    x_other = core(x_mine)
    a_factor = gram_rows(x_mine, [x_column], mine_at, scale, rows_all)
    a_factor = gram_rows(x_other, [x_column], other_at, scale, rows_all, a_factor)
    return a_factor, g_factor


def solution(mesh):
    square = mesh.shape["dp"] == 8 and mesh.shape["ctx"] == 4
    return jax.shard_map(
        square_plane if square else general,
        mesh=mesh,
        in_specs=(P("ctx", "dp"), P("ctx", "dp"), P(None, "dp")),
        out_specs=(P("ctx", "dp"), P("ctx", "dp")),
        check_vma=False,
    )
```
